32 devices in a mesh: dp: 8 (over z, y), head: 4 (over x, core).
Axes of the slice: x: 2, y: 2, z: 4, core: 2. Of those that a mesh axis runs over, the one named last changes fastest.
Arguments:
- tokens: bfloat16 [131072, 512], P(('dp', 'head')), may hold values from -6 to 6
- lengths: int32 [128], P('dp'), may hold values from 512 to 1024, as said below
- feature_proj: float32 [8, 64, 128], replicated, may hold values from -0.75 to 0.75
- first_gain: bfloat16 [512], P(('dp', 'head')), may hold values from 0.5 to 1.5
- query_weight: bfloat16 [512, 512], P(('dp', 'head')), may hold values from -0.25 to 0.25
- key_weight: bfloat16 [512, 512], P(('dp', 'head')), may hold values from -0.25 to 0.25
- value_weight: bfloat16 [512, 512], P(('dp', 'head')), may hold values from -0.25 to 0.25
- gate_weight: bfloat16 [512, 8], P(('dp', 'head')), may hold values from -0.25 to 0.25
- gate_bias: float32 [8], replicated, may hold values from -1 to 7
- output_weight: bfloat16 [512, 512], P(('dp', 'head')), may hold values from -1 to 1
- second_gain: bfloat16 [512], P(('dp', 'head')), may hold values from 0.5 to 1.5
- up_weight: bfloat16 [512, 2048], P(('dp', 'head')), may hold values from -0.25 to 0.25
- down_weight: bfloat16 [2048, 512], P(('dp', 'head')), may hold values from -0.125 to 0.125
- cotangent: bfloat16 [131072, 512], P(('dp', 'head')), may hold values from -6 to 6
Outputs:
- mixed: bfloat16 [131072, 512], P(('dp', 'head'))
- grad_tokens: float32 [131072, 512], P(('dp', 'head'))
- grad_first_gain: float32 [512], P(('dp', 'head'))
- grad_query: float32 [512, 512], P(('dp', 'head'))
- grad_key: float32 [512, 512], P(('dp', 'head'))
- grad_value: float32 [512, 512], P(('dp', 'head'))
- grad_gate_weight: float32 [512, 8], P(('dp', 'head'))
- grad_gate_bias: float32 [8], replicated
- grad_output: float32 [512, 512], P(('dp', 'head'))
- grad_second_gain: float32 [512], P(('dp', 'head'))
- grad_up: float32 [512, 2048], P(('dp', 'head'))
- grad_down: float32 [2048, 512], P(('dp', 'head'))
The draws below stay inside these ranges and needn't reach their ends.
Inputs may be any that keep to these rules, and one draw needn't show every extreme that they name: `lengths`: in every aligned block of 16 entries (the sentences of one index of dp) one entry equals 1024.
All inputs are finite; a program needn't handle non-finite values.
Results may differ from the reference program's by a relative error of at most 0.012.
Values may be sent and summed in bfloat16 or wider, within the bound.
No kernel may reach another device: no remote copies, remote signals or barrier semaphores. Data moves between devices by JAX's collectives and lax.ppermute only.
A program may use at most 704 MiB of HBM per device.

```python
import math
import jax
import jax.numpy as jnp
from jax import lax

HEADS = 8
HD = 64
D = 512
FF = 2048
FEAT = 128
BLOCK = 128
SENT_LEN = 1024
SLOTS = 16
PIECE = 256
TOKENS = 131072
SENTS = 128
N_DP = 8
N_HEAD = 4


def draw_lengths(key, part):
    key = jax.random.fold_in(key, 11)
    first_key, second_key = jax.random.split(key)
    groups = SENTS // SLOTS
    drawn = jax.random.randint(first_key, (groups, SLOTS), SENT_LEN // 2, SENT_LEN + 1, dtype=jnp.int32)
    chosen = jax.random.randint(second_key, (groups, 1), 0, SLOTS, dtype=jnp.int32)
    slot_ids = jnp.arange(SLOTS, dtype=jnp.int32)[None, :]
    return jnp.where(slot_ids == chosen, SENT_LEN, drawn).reshape(SENTS)


def shard_levels(stream_key, extent, pieces, smallest, high):
    factor_of = 1.0
    for position, parts in pieces:
        steps = jax.random.uniform(jax.random.fold_in(jax.random.fold_in(stream_key, 6), position), (parts,), jnp.float32, smallest / len(pieces), high / len(pieces))
        factor_of = factor_of * jnp.repeat(jnp.exp(steps), extent[position] // parts).reshape((-1,) + (1,) * (len(extent) - 1 - position))
    return factor_of


def scatter_about(key, extent, width, reach, cuts=(), kind=jnp.bfloat16):
    values = jax.random.normal(key, extent, jnp.float32) * width
    if len(cuts) > 0:
        values = shard_levels(key, extent, cuts, -0.22, 0.18) * values
    return jnp.clip(values, min=-reach, max=reach).astype(kind)


def setup_inputs(seed: int = 0) -> dict:
    seeds = jax.random.split(jax.random.key(seed), 15)
    return {
        "tokens": scatter_about(seeds[0], (TOKENS, D), 1.0, 6.0, ((0, 32),)),
        "lengths": draw_lengths(jax.random.fold_in(seeds[14], 71), 0),
        "feature_proj": scatter_about(seeds[2], (HEADS, HD, FEAT), HD ** -0.5, 0.75, (), jnp.float32),
        "first_gain": jnp.clip(1.0 + 0.1 * jax.random.normal(seeds[3], (D,), jnp.float32), 0.5, 1.5).astype(jnp.bfloat16),
        "query_weight": scatter_about(seeds[4], (D, D), D ** -0.5, 0.25, ((0, 32),)),
        "key_weight": scatter_about(seeds[5], (D, D), D ** -0.5, 0.25, ((0, 32),)),
        "value_weight": scatter_about(seeds[6], (D, D), D ** -0.5, 0.25, ((0, 32),)),
        "gate_weight": scatter_about(seeds[7], (D, HEADS), D ** -0.5, 0.25, ((0, 32),)),
        "gate_bias": jnp.clip(jax.random.uniform(seeds[8], (HEADS,), jnp.float32, -1.0, 7.0), -1.0, 7.0),
        "output_weight": scatter_about(seeds[9], (D, D), (D // 16) ** -0.5, 1.0, ((0, 32),)),
        "second_gain": jnp.clip(1.0 + 0.1 * jax.random.normal(seeds[10], (D,), jnp.float32), 0.5, 1.5).astype(jnp.bfloat16),
        "up_weight": scatter_about(seeds[11], (D, FF), D ** -0.5, 0.25, ((0, 32),)),
        "down_weight": scatter_about(seeds[12], (FF, D), FF ** -0.5, 0.125, ((0, 32),)),
        "cotangent": scatter_about(seeds[13], (TOKENS, D), 1.0, 6.0, ((0, 32),)),
    }


norm_eps = 1e-05
floor_sq = 0.01
highest = lax.Precision.HIGHEST

@jax.custom_vjp
def low(v):
    return lax.optimization_barrier(v.astype(jnp.bfloat16)).astype(jnp.float32)

@jax.custom_vjp
def low_back(v):
    return v

def low_keep(v):
    return (low(v), None)

def low_pass(kept, grad):
    return (grad,)

def back_keep(v):
    return (v, None)

def back_low(kept, grad):
    return (low(grad),)
low.defvjp(low_keep, low_pass)
low_back.defvjp(back_keep, back_low)

def both_ways(values):
    return low_back(low(values))

def product(left, right):
    return jnp.dot(left, right, precision=highest, preferred_element_type=jnp.float32)

def layer_norm(rows_in, gain_row):
    center = rows_in - lax.optimization_barrier(jnp.mean(rows_in, axis=-1, keepdims=True))
    spread = lax.optimization_barrier(jnp.mean(center * center, axis=-1, keepdims=True))
    return center * lax.rsqrt(spread + norm_eps) * gain_row

def random_features(inputs, projection):
    angles = jnp.einsum('lhd,hdf->lhf', inputs, projection, precision=highest)
    scale_factor = 1.0 / math.sqrt(projection.shape[2])
    return jnp.concatenate([jnp.sin(angles), jnp.cos(angles)], axis=-1) * scale_factor

def gated_state(queries, key_rows, values, logits, projection, block_len):
    total_len, head_count, head_size = queries.shape
    span_count = total_len // block_len
    phi_query = random_features(queries, projection).reshape(span_count, block_len, head_count, -1)
    phi_key = random_features(key_rows, projection).reshape(span_count, block_len, head_count, -1)
    value_blocks = values.reshape(span_count, block_len, head_count, head_size)
    log_gate = -jax.nn.softplus(-logits).reshape(span_count, block_len, head_count)
    write_rate = jax.nn.sigmoid(-logits).reshape(span_count, block_len, head_count)
    cum_gate = jnp.cumsum(log_gate, axis=1)
    row_ids = jnp.arange(block_len)
    causal = (row_ids[:, None] >= row_ids[None, :])[None, :, :, None]
    gap_log = cum_gate[:, :, None, :] - cum_gate[:, None, :, :]
    decay_mat = jnp.exp(jnp.where(causal, gap_log, -1e+30)) * write_rate[:, None, :, :]
    scores = jnp.einsum('cthf,cjhf->ctjh', phi_query, phi_key, precision=highest) * decay_mat
    numer_part = jnp.einsum('ctjh,cjhd->cthd', scores, value_blocks, precision=highest)
    denom_part = lax.optimization_barrier(jnp.sum(scores, axis=2))
    tail_weight = (jnp.exp(cum_gate[:, -1:, :] - cum_gate) * write_rate)[..., None] * phi_key
    span_state = jnp.einsum('cjhf,cjhd->chfd', tail_weight, value_blocks, precision=highest)
    span_norm = lax.optimization_barrier(jnp.sum(tail_weight, axis=1))
    span_decay = jnp.exp(cum_gate[:, -1, :])

    def carry_step(carried, inputs):
        state_prev, norm_prev = carried
        add_state, add_norm, keep_rate = inputs
        following = (keep_rate[:, None, None] * state_prev + add_state, keep_rate[:, None] * norm_prev + add_norm)
        return (following, (state_prev, norm_prev))
    feature_count = phi_key.shape[-1]
    initial = (jnp.zeros((head_count, feature_count, head_size), jnp.float32), jnp.zeros((head_count, feature_count), jnp.float32))
    ignored, (state_in, norm_in) = lax.scan(carry_step, initial, (span_state, span_norm, span_decay))
    lead_decay = jnp.exp(cum_gate)
    numer_part = numer_part + lead_decay[..., None] * jnp.einsum('cthf,chfd->cthd', phi_query, state_in, precision=highest)
    denom_part = denom_part + lead_decay * jnp.einsum('cthf,chf->cth', phi_query, norm_in, precision=highest)
    attended = numer_part * lax.rsqrt(denom_part * denom_part + floor_sq)[..., None]
    return attended.reshape(total_len, head_count, head_size)

def reference(tokens, lengths, feature_proj, first_gain, query_weight, key_weight, value_weight, gate_weight, gate_bias, output_weight, second_gain, up_weight, down_weight, cotangent):
    sent_count = N_DP * SLOTS

    def reorder(rows_in):
        wide = rows_in.shape[-1]
        shaped = rows_in.reshape(N_DP, N_HEAD, SLOTS, PIECE, wide)
        return shaped.transpose(0, 2, 1, 3, 4).reshape(sent_count, SENT_LEN, wide)

    def restore(sent_rows):
        wide = sent_rows.shape[-1]
        shaped = sent_rows.reshape(N_DP, SLOTS, N_HEAD, PIECE, wide)
        return shaped.transpose(0, 2, 1, 3, 4).reshape(TOKENS, wide)
    live_mask = (jnp.arange(SENT_LEN, dtype=jnp.int32)[None, :] < lengths[:, None]).astype(jnp.float32)

    def one_sentence(packed):
        query_one, key_one, value_one, logit_one = packed
        result = gated_state(query_one.reshape(SENT_LEN, HEADS, HD), key_one.reshape(SENT_LEN, HEADS, HD), value_one.reshape(SENT_LEN, HEADS, HD), logit_one, feature_proj, BLOCK)
        return result.reshape(SENT_LEN, D)

    def forward(inputs, gain_one, query_full, key_full, value_full, gate_full, bias_full, output_full, gain_two, up_full, down_full):
        normed_one = low(layer_norm(inputs, gain_one))
        queries = both_ways(product(normed_one, query_full))
        key_rows = both_ways(product(normed_one, key_full))
        value_rows = both_ways(product(normed_one, value_full))
        logits = both_ways(product(normed_one, gate_full) + bias_full)
        mapped = lax.map(jax.checkpoint(one_sentence), (reorder(queries), reorder(key_rows), reorder(value_rows), reorder(logits)))
        heads_low = both_ways(restore(mapped * live_mask[:, :, None]))
        middle = inputs + low_back(product(heads_low, output_full))
        normed_two = low(layer_norm(middle, gain_two))
        hidden_pre = low_back(product(normed_two, up_full))
        hidden_low = low(jax.nn.gelu(hidden_pre))
        return middle + product(hidden_low, down_full)
    primal = (tokens.astype(jnp.float32), first_gain.astype(jnp.float32), query_weight.astype(jnp.float32), key_weight.astype(jnp.float32), value_weight.astype(jnp.float32), gate_weight.astype(jnp.float32), gate_bias.astype(jnp.float32), output_weight.astype(jnp.float32), second_gain.astype(jnp.float32), up_weight.astype(jnp.float32), down_weight.astype(jnp.float32))
    result, pull = jax.vjp(forward, primal[0], primal[1], primal[2], primal[3], primal[4], primal[5], primal[6], primal[7], primal[8], primal[9], primal[10])
    grads = pull(cotangent.astype(jnp.float32))
    return (result.astype(jnp.bfloat16), grads[0], grads[1], grads[2], grads[3], grads[4], grads[5], grads[6], grads[7], grads[8], grads[9], grads[10])
```

```python
import functools
import math

import jax
import jax.numpy as jnp
from jax import lax
from jax.experimental import pallas as pl
from jax.experimental.pallas import tpu as pltpu
from jax.sharding import PartitionSpec as P

HEADS = 8
HD = 64
FEAT = 128
PHI = 2 * FEAT
PAIRS = HEADS // 2
TILE = 128
STATE_ROWS = HEADS * HD + 16

norm_eps = 1e-05
floor_sq = 0.01
f32 = jnp.float32
bf16 = jnp.bfloat16

ROOT_2_PI = math.sqrt(2.0 / math.pi)


def dot(left, right):
    return jnp.dot(left, right, preferred_element_type=f32)


def dot_t(left, right):
    return lax.dot_general(left, right, (((1,), (1,)), ((), ())), preferred_element_type=f32)


def t_dot(left, right):
    return lax.dot_general(left, right, (((0,), (0,)), ((), ())), preferred_element_type=f32)


def sincos_turns(turns):
    r = turns - jnp.round(turns)
    s = r * r
    half_sin = r * (4.4428679 + s * (-7.30744346 + s * (3.59478832 + s * -0.78437455)))
    half_cos = 1.41420413 + s * (-6.9776436 + s * (5.71525082 + s * -1.72837716))
    return half_sin * half_cos, 1.0 - half_sin * half_sin


def exact_sum(mask, values):
    high = values.astype(bf16)
    rest = values - high.astype(f32)
    mid = rest.astype(bf16)
    low = (rest - mid.astype(f32)).astype(bf16)
    return dot(mask, high) + dot(mask, mid) + dot(mask, low)


def iota(shape, axis):
    return lax.broadcasted_iota(jnp.int32, shape, axis)


def tiles_of(rows, step):
    return [slice(r, r + step) for r in range(0, rows, step)]


def pair_masks(rows):
    lane = iota((rows, TILE), 1)
    return lane < HD, lane >= HD


def whole_spec(array):
    shape = array.shape
    return pl.BlockSpec(shape, lambda i, *_: (0,) * len(shape))


def row_spec(block, first):
    rest = (0,) * (len(block) - 1)
    return pl.BlockSpec(block, lambda i, *_: (i + first,) + rest)


ANY_SPEC = pl.BlockSpec(memory_space=pl.ANY)


def staged_call(kernel, name, steps, ins, in_specs, outs, out_specs, kept, after, flops, moved,
                scratch=(), prefetch=()):
    extra = list(kept) + list(after)
    head = len(prefetch) + len(ins)

    def trimmed(*refs):
        kernel(*refs[:head], *refs[head + len(extra):])

    return pl.pallas_call(
        trimmed,
        grid_spec=pltpu.PrefetchScalarGridSpec(
            num_scalar_prefetch=len(prefetch),
            grid=(steps,),
            in_specs=list(in_specs) + [ANY_SPEC] * len(extra),
            out_specs=list(out_specs),
            scratch_shapes=list(scratch),
        ),
        out_shape=list(outs),
        input_output_aliases={head + j: j for j in range(len(kept))},
        compiler_params=pltpu.CompilerParams(vmem_limit_bytes=60 * 2**20),
        cost_estimate=pl.CostEstimate(flops=flops, bytes_accessed=moved, transcendentals=0),
        name=name,
    )(*prefetch, *ins, *extra)


def merged_state(index, odd, arrivals, out_ref):
    near_ref, cross_ref, swap_ref = arrivals

    def both(rows):
        cross = cross_ref[index, rows, :].astype(f32)
        swapped = swap_ref[index, rows, :].astype(f32)
        return jnp.where(odd, swapped, cross), jnp.where(odd, cross, swapped)

    block = slice(HEADS * HD, STATE_ROWS)
    near = near_ref[index, block, :].astype(f32)
    second, first = both(block)
    keep_second = second[8:16]
    keep_near = jnp.where(odd, near[8:16], 1.0)
    for head in range(HEADS):
        rows = slice(head * HD, (head + 1) * HD)
        state, older = both(rows)
        state = state + keep_second[head:head + 1] * older
        out_ref[index, rows, :] = (near_ref[index, rows, :].astype(f32)
                                   + keep_near[head:head + 1] * state).astype(bf16)
    norm = near[0:8] + keep_near * (second[0:8] + keep_second * first[0:8])
    out_ref[index, block, :] = jnp.concatenate([norm, jnp.zeros_like(norm)], axis=0).astype(bf16)


def join_kernel(own_ref, came_ref, out_ref):
    for i in range(own_ref.shape[0]):
        block = slice(HEADS * HD, STATE_ROWS)
        own = own_ref[i, block, :].astype(f32)
        came = came_ref[i, block, :].astype(f32)
        keep = own[8:16]
        for head in range(HEADS):
            rows = slice(head * HD, (head + 1) * HD)
            out_ref[i, rows, :] = (own_ref[i, rows, :].astype(f32)
                                   + keep[head:head + 1] * came_ref[i, rows, :].astype(f32)).astype(bf16)
        out_ref[i, block, :] = jnp.concatenate(
            [own[0:8] + keep * came[0:8], keep * came[8:16]], axis=0).astype(bf16)


def join_states(own, came):
    steps = 2
    spec = row_spec((own.shape[0] // steps,) + own.shape[1:], 0)
    return staged_call(join_kernel, "join", steps, [own, came], [spec, spec],
                       [jax.ShapeDtypeStruct(own.shape, bf16)], [spec], (), (),
                       own.size * 4, own.size * 6)[0]


def write_features(source, proj_ref, out_ref):
    for pair in range(PAIRS):
        part = source[:, pair * TILE:(pair + 1) * TILE]
        angle = dot(jnp.concatenate([part, part], axis=1), proj_ref[pair])
        start = 2 * pair * PHI
        for tile in tiles_of(source.shape[0], 64):
            sine, cosine = sincos_turns(angle[tile])
            sine = sine.astype(bf16)
            cosine = cosine.astype(bf16)
            out_ref[tile, start:start + FEAT] = sine[:, :FEAT]
            out_ref[tile, start + FEAT:start + 2 * FEAT] = cosine[:, :FEAT]
            out_ref[tile, start + 2 * FEAT:start + 3 * FEAT] = sine[:, FEAT:]
            out_ref[tile, start + 3 * FEAT:start + 4 * FEAT] = cosine[:, FEAT:]


def key_kernel(piece, x_ref, gain_ref, w_ref, bias_ref, proj_ref,
               n_ref, pk_ref, v_ref, gc_ref, gr_ref, st_ref):
    total, width = x_ref.shape
    gain = gain_ref[...]
    for tile in tiles_of(total, 128):
        x = x_ref[tile, :].astype(f32)
        center = x - jnp.mean(x, axis=1, keepdims=True)
        spread = jnp.mean(center * center, axis=1, keepdims=True)
        n_ref[tile, :] = (center * lax.rsqrt(spread + norm_eps) * gain).astype(bf16)
    normed = n_ref[...]
    logits = (dot(normed, w_ref[:, 3 * width:]) + bias_ref[...]).astype(bf16).astype(f32)
    soft = jnp.log1p(jnp.exp(-jnp.abs(logits)))
    log_gate = jnp.minimum(logits, 0.0) - soft
    log_write = -jnp.maximum(logits, 0.0) - soft
    keys = dot(normed, w_ref[:, width:2 * width]).astype(bf16)
    values = dot(normed, w_ref[:, 2 * width:3 * width]).astype(bf16)
    v_ref[...] = values
    lower = (iota((piece, piece), 0) >= iota((piece, piece), 1)).astype(bf16)
    lane = iota((piece, TILE), 1)
    count = total // piece
    tails = []
    keeps = []
    for i in range(count):
        rows = slice(i * piece, (i + 1) * piece)
        cum = exact_sum(lower, log_gate[rows])
        delay = cum - log_write[rows] + math.log(FEAT)
        packed = jnp.where(lane < 8, cum, jnp.where(lane < 16, delay, logits[rows]))
        gc_ref[rows, :] = packed
        turned = packed.T
        gr_ref[i] = turned[0:16]
        last = turned[0:8, piece - 1:piece]
        tails.append(jnp.exp(last - turned[8:16]))
        keeps.append(jnp.broadcast_to(jnp.exp(last), (8, PHI)))
    write_features(keys, proj_ref, pk_ref)
    sub = iota((8, PHI), 0)
    for i in range(count):
        rows = slice(i * piece, (i + 1) * piece)
        norm_rows = jnp.zeros((8, PHI), f32)
        tail_low = jnp.concatenate([tails[i], jnp.zeros_like(tails[i])], axis=0).astype(bf16)
        for pair in range(PAIRS):
            turned = values[rows, pair * TILE:(pair + 1) * TILE].astype(f32).T
            for side in range(2):
                head = 2 * pair + side
                scaled = (turned[side * HD:(side + 1) * HD] * tails[i][head:head + 1]).astype(bf16)
                left = jnp.concatenate([scaled, tail_low], axis=0)
                state = dot(left, pk_ref[rows, head * PHI:(head + 1) * PHI])
                st_ref[i, head * HD:(head + 1) * HD, :] = state[0:HD].astype(bf16)
                norm_rows = jnp.where(sub == head, state[HD:HD + 8], norm_rows)
        st_ref[i, HEADS * HD:STATE_ROWS, :] = jnp.concatenate([norm_rows, keeps[i]], axis=0).astype(bf16)


def key_call(x, gain, weights, gate_b, proj, piece, per, sents, first, kept, after):
    total, width = x.shape
    all_sents = total // piece
    tall = lambda cols: row_spec((per * piece, cols), first // per)
    return staged_call(
        functools.partial(key_kernel, piece), "keys", sents // per,
        [x, gain, weights, gate_b, proj],
        [tall(width)] + [whole_spec(a) for a in (gain, weights, gate_b, proj)],
        [
            jax.ShapeDtypeStruct((total, width), bf16),
            jax.ShapeDtypeStruct((total, HEADS * PHI), bf16),
            jax.ShapeDtypeStruct((total, width), bf16),
            jax.ShapeDtypeStruct((total, TILE), f32),
            jax.ShapeDtypeStruct((all_sents, 16, piece), f32),
            jax.ShapeDtypeStruct((sents, STATE_ROWS, PHI), bf16),
        ],
        [tall(width), tall(HEADS * PHI), tall(width), tall(TILE),
         row_spec((per, 16, piece), first // per), row_spec((per, STATE_ROWS, PHI), 0)],
        kept, after, 2 * sents * piece * width * 3 * width * 3, sents * piece * HEADS * PHI * 3)


def query_kernel(n_ref, w_ref, proj_ref, pq_ref):
    width = n_ref.shape[1]
    write_features(dot(n_ref[...], w_ref[:, 0:width]).astype(bf16), proj_ref, pq_ref)


def query_call(n, weights, proj, after):
    total, width = n.shape
    rows = min(512, total)
    return staged_call(
        query_kernel, "queries", total // rows, [n, weights, proj],
        [row_spec((rows, width), 0), whole_spec(weights), whole_spec(proj)],
        [jax.ShapeDtypeStruct((total, HEADS * PHI), bf16)], [row_spec((rows, HEADS * PHI), 0)], (), after,
        total * width * width, total * width)


def staggered(units, stages, stagger):
    if not stagger:
        for unit in units:
            for stage in stages:
                stage(*unit)
        return
    for turn in range(len(units) + len(stages) - 1):
        for place, stage in enumerate(stages):
            if 0 <= turn - place < len(units):
                stage(*units[turn - place])


def pick(side_even, first, second):
    return jnp.where(side_even, first, second)


def state_pair(st_ref, index, pair):
    even = 2 * pair
    top = st_ref[index, even * HD:(even + 1) * HD, :]
    bottom = st_ref[index, (even + 1) * HD:(even + 2) * HD, :]
    base = HEADS * HD
    block = st_ref[index, base:STATE_ROWS, :].astype(f32)
    norm_even = jnp.broadcast_to(block[even:even + 1], (HD, PHI)).astype(bf16)
    norm_odd = jnp.broadcast_to(block[even + 1:even + 2], (HD, PHI)).astype(bf16)
    return top, bottom, norm_even, norm_odd


def middle_kernel(piece, first_sent, stagger, cuts, bound_ref, x_ref, cot_ref, pq_ref, pk_ref, v_ref, gc_ref, gr_ref,
                  near_ref, far_ref, late_ref, gain_ref, w_ref, seg_ref,
                  mixed_ref, gm_ref, heads_ref, n_ref, act_ref, gpre_ref, dn_ref, st_ref, *rest):
    ad_ref, numer_ref, den_ref, mid_ref, hat_ref, low_ref = rest[len(cuts):]
    step = pl.program_id(0)
    total, width = x_ref.shape
    hidden = act_ref.shape[1]
    count = total // piece
    tiles = piece // TILE
    even_lane, odd_lane = pair_masks(piece)
    ones_even = even_lane.astype(bf16)
    ones_odd = odd_lane.astype(bf16)
    diag = iota((TILE, TILE), 0) >= iota((TILE, TILE), 1)
    zero_tile = jnp.zeros((TILE, TILE), bf16)
    units = [(i, pair) for i in range(count) for pair in range(PAIRS)]
    held = {}

    def span(i):
        return slice(i * piece, (i + 1) * piece)

    def start(i, pair):
        rows = span(i)
        scores = []
        for side in range(2):
            head = 2 * pair + side
            feats = slice(head * PHI, (head + 1) * PHI)
            scores.append(dot_t(pq_ref[rows, feats], pk_ref[rows, feats]))
        top, bottom, norm_even, norm_odd = state_pair(st_ref, i, pair)
        blank = jnp.zeros((HD, PHI), bf16)
        carried = jnp.concatenate([
            jnp.concatenate([top, blank], axis=1), jnp.concatenate([blank, bottom], axis=1),
            jnp.concatenate([norm_even, blank], axis=1),
            jnp.concatenate([blank, norm_odd], axis=1)], axis=0)
        outer = dot_t(pq_ref[rows, 2 * pair * PHI:(2 * pair + 2) * PHI], carried)
        held[i, pair] = scores, outer

    def weigh(i, pair):
        scores, outer = held[i, pair]
        lefts = []
        for side in range(2):
            head = 2 * pair + side
            lines = []
            for a in range(tiles):
                lead = gc_ref[i * piece + a * TILE:i * piece + (a + 1) * TILE, head:head + 1]
                line = []
                for b in range(tiles):
                    if b > a:
                        line.append(zero_tile)
                        continue
                    gap = lead - gr_ref[i, 8 + head:9 + head, b * TILE:(b + 1) * TILE]
                    if a == b:
                        gap = jnp.where(diag, gap, -1e30)
                    part = scores[side][a * TILE:(a + 1) * TILE, b * TILE:(b + 1) * TILE]
                    line.append((jnp.exp(gap) * part).astype(bf16))
                lines.append(jnp.concatenate(line, axis=1))
            lefts.append(jnp.concatenate(lines, axis=0))
        held[i, pair] = lefts, outer

    def mix(i, pair):
        lefts, outer = held[i, pair]
        value = v_ref[span(i), pair * TILE:(pair + 1) * TILE]
        right = jnp.concatenate([
            jnp.concatenate([value * ones_even, ones_even], axis=1),
            jnp.concatenate([value * ones_odd, ones_odd], axis=1)], axis=0)
        held[i, pair] = dot(jnp.concatenate(lefts, axis=1), right), outer

    def attend(i, pair):
        inner, outer = held.pop((i, pair))
        cols = slice(pair * TILE, (pair + 1) * TILE)
        bound = bound_ref[first_sent + step * count + i]
        for tile in tiles_of(piece, TILE):
            rows = slice(i * piece + tile.start, i * piece + tile.stop)
            lead = jnp.exp(pick(even_lane[tile], gc_ref[rows, 2 * pair:2 * pair + 1],
                                gc_ref[rows, 2 * pair + 1:2 * pair + 2]))
            numer = inner[tile, :TILE] + lead * outer[tile, :TILE]
            den = inner[tile, TILE:] + lead * outer[tile, TILE:]
            numer_ref[rows, cols] = numer
            den_ref[rows, cols] = den
            attended = numer * lax.rsqrt(den * den + floor_sq)
            live = iota((TILE, TILE), 0) < bound - tile.start
            heads_ref[rows, cols] = jnp.where(live, attended, 0.0).astype(bf16)

    for i in range(count):
        merged_state(i, bound_ref[bound_ref.shape[0] - 1] > 0, (near_ref, far_ref, late_ref), st_ref)
    staggered(units, [start, weigh, mix, attend], stagger)

    proj = dot(heads_ref[...], w_ref[:, hidden:hidden + width])
    gain = gain_ref[...]
    scales = []
    for tile in tiles_of(total, 128):
        middle = x_ref[tile, :].astype(f32) + proj[tile]
        center = middle - jnp.mean(middle, axis=1, keepdims=True)
        spread = jnp.mean(center * center, axis=1, keepdims=True)
        scale = lax.rsqrt(spread + norm_eps)
        xhat = center * scale
        mid_ref[tile, :] = middle
        hat_ref[tile, :] = xhat
        scales.append(scale)
        n_ref[tile, :] = (xhat * gain).astype(bf16)
    normed = n_ref[...]
    cot = cot_ref[...]
    chunks = list(range(hidden // width))

    def chunk_cols(c):
        return (slice(c * width, (c + 1) * width),
                slice(hidden + (c + 1) * width, hidden + (c + 2) * width))

    def raise_up(c):
        cols, down_cols = chunk_cols(c)
        held[c] = dot(normed, w_ref[:, cols]), dot_t(cot, w_ref[:, down_cols])

    def activate(c):
        cols, _ = chunk_cols(c)
        all_pre, all_back = held.pop(c)
        for tile in tiles_of(total, 32):
            pre = all_pre[tile]
            square = pre * pre
            th = jnp.tanh(pre * (ROOT_2_PI + (ROOT_2_PI * 0.044715) * square))
            half = 0.5 + 0.5 * th
            slope = half + (pre * (half - half * half)) * (
                2.0 * ROOT_2_PI + (6.0 * ROOT_2_PI * 0.044715) * square)
            act_ref[tile, cols] = (pre * half).astype(bf16)
            gpre_ref[tile, cols] = (slope * all_back[tile]).astype(bf16)

    def bring_down(c):
        cols, down_cols = chunk_cols(c)
        mixed = dot(act_ref[:, cols], w_ref[:, down_cols])
        grad_n = dot_t(gpre_ref[:, cols], w_ref[:, cols])
        if "sums" in held:
            mixed = held["sums"][0] + mixed
            grad_n = held["sums"][1] + grad_n
        held["sums"] = mixed, grad_n

    staggered([(c,) for c in chunks], [raise_up, activate, bring_down], stagger)
    mixed, grad_n = held.pop("sums")
    for number, tile in enumerate(tiles_of(total, 128)):
        mixed_ref[tile, :] = (mid_ref[tile, :] + mixed[tile]).astype(bf16)
        xhat = hat_ref[tile, :]
        gy = grad_n[tile] * gain
        first = jnp.mean(gy, axis=1, keepdims=True)
        second = jnp.mean(gy * xhat, axis=1, keepdims=True)
        grad_m = cot_ref[tile, :].astype(f32) + scales[number] * (gy - first - xhat * second)
        gm_ref[tile, :] = grad_m
        low_ref[tile, :] = grad_m.astype(bf16)
    grad_h = dot_t(low_ref[...], w_ref[:, hidden:hidden + width])
    sub = iota((8, PHI), 0)

    def divide(i, pair):
        cols = slice(pair * TILE, (pair + 1) * TILE)
        bound = bound_ref[first_sent + step * count + i]
        grads = []
        sums = []
        for tile in tiles_of(piece, TILE):
            rows = slice(i * piece + tile.start, i * piece + tile.stop)
            live = iota((TILE, TILE), 0) < bound - tile.start
            grad = jnp.where(live, grad_h[rows, cols], 0.0).astype(bf16).astype(f32)
            den = den_ref[rows, cols]
            inv = lax.rsqrt(den * den + floor_sq)
            dn = grad * inv
            along = dn * numer_ref[rows, cols]
            high = along.astype(bf16)
            low = (along - high.astype(f32)).astype(bf16)
            dn_ref[rows, 2 * pair * TILE:(2 * pair + 1) * TILE] = dn.astype(bf16)
            grads.append(dn)
            sums.append(jnp.concatenate([high, low], axis=1))
        seg = dot(jnp.concatenate(sums, axis=0), seg_ref[...])
        held[i, pair] = jnp.concatenate(grads, axis=0), seg

    def gather_state(i, pair):
        dn, seg = held.pop((i, pair))
        cols = slice(pair * TILE, (pair + 1) * TILE)
        grads = []
        for tile in tiles_of(piece, TILE):
            rows = slice(i * piece + tile.start, i * piece + tile.stop)
            den = den_ref[rows, cols]
            inv = lax.rsqrt(den * den + floor_sq)
            dd = -(seg[tile] * (den * (inv * inv)))
            dn_ref[rows, (2 * pair + 1) * TILE:(2 * pair + 2) * TILE] = dd.astype(bf16)
            grads.append(dd)
        turned = dn.T
        turned_d = jnp.concatenate(grads, axis=0).T
        lead_rows = jnp.exp(gr_ref[i, 0:8, :])
        if pair == 0:
            held["norm", i] = jnp.zeros((8, PHI), f32)
        for side in range(2):
            head = 2 * pair + side
            lead = lead_rows[head:head + 1]
            left = jnp.concatenate([turned[side * HD:(side + 1) * HD] * lead,
                                    turned_d[side * HD:side * HD + 16] * lead], axis=0)
            state = dot(left.astype(bf16), pq_ref[span(i), head * PHI:(head + 1) * PHI])
            ad_ref[i, head * HD:(head + 1) * HD, :] = state[0:HD].astype(bf16)
            held["norm", i] = jnp.where(sub == head, state[HD:HD + 8], held["norm", i])
        if pair == PAIRS - 1:
            keep = jnp.broadcast_to(lead_rows[:, piece - 1:piece], (8, PHI))
            ad_ref[i, HEADS * HD:STATE_ROWS, :] = jnp.concatenate(
                [held.pop(("norm", i)), keep], axis=0).astype(bf16)

    staggered(units, [divide, gather_state], stagger)
    for out_ref, (low, high) in zip(rest, cuts):
        @pl.when((step >= low // count) & (step < high // count))
        def _(out_ref=out_ref):
            out_ref[...] = ad_ref[...]


def middle_call(bound, x, cot, pq, pk, v, gc, gr, arrivals, gain, weights, seg, piece, per, form, cuts, sents, first,
                kept, after):
    total, width = x.shape
    hidden = (weights.shape[1] - width) // 2
    all_sents = total // piece
    tall = lambda cols: row_spec((per * piece, cols), first // per)
    state = row_spec((per, STATE_ROWS, PHI), 0)
    return staged_call(
        functools.partial(middle_kernel, piece, first, form, cuts), "middle", sents // per,
        [x, cot, pq, pk, v, gc, gr, *arrivals, gain, weights, seg],
        [tall(width), tall(width), tall(HEADS * PHI), tall(HEADS * PHI), tall(width), tall(TILE),
         row_spec((per, 16, piece), first // per), state, state, state]
        + [whole_spec(a) for a in (gain, weights, seg)],
        [
            jax.ShapeDtypeStruct((total, width), bf16),
            jax.ShapeDtypeStruct((total, width), f32),
            jax.ShapeDtypeStruct((total, width), bf16),
            jax.ShapeDtypeStruct((total, width), bf16),
            jax.ShapeDtypeStruct((total, hidden), bf16),
            jax.ShapeDtypeStruct((total, hidden), bf16),
            jax.ShapeDtypeStruct((total, 2 * width), bf16),
            jax.ShapeDtypeStruct((all_sents, STATE_ROWS, PHI), bf16),
            *(jax.ShapeDtypeStruct((high - low, STATE_ROWS, PHI), bf16) for low, high in cuts),
        ],
        [tall(width), tall(width), tall(width), tall(width), tall(hidden), tall(hidden),
         tall(2 * width), row_spec((per, STATE_ROWS, PHI), first // per),
         *(part_spec((per, STATE_ROWS, PHI), low // per, high // per) for low, high in cuts)],
        kept, after, sents * piece * width * TILE, sents * piece * TILE,
        scratch=[pltpu.VMEM((per, STATE_ROWS, PHI), bf16)] + [pltpu.VMEM((per * piece, width), f32)] * 4 + [pltpu.VMEM((per * piece, width), bf16)],
        prefetch=[bound])


def mlp_grad_kernel(n_ref, gpre_ref, act_ref, cot_ref, heads_ref, gm_ref, out_ref, down_ref):
    step = pl.program_id(0)
    width = n_ref.shape[1]
    wide = act_ref.shape[1] // width
    parts = out_ref.shape[0]
    share = width // parts

    @pl.when(step == 0)
    def _():
        down_ref[...] = jnp.zeros_like(down_ref)
        out_ref[...] = jnp.zeros_like(out_ref)

    normed = n_ref[...].T
    cot = cot_ref[...].T
    for c in range(wide):
        cols = slice(c * width, (c + 1) * width)
        lines = slice((wide + c) * share, (wide + c + 1) * share)
        out_ref[:, lines, :] += dot(normed, gpre_ref[:, cols]).reshape(parts, share, width)
        down_ref[:, cols] += dot(cot, act_ref[:, cols])
    out_ref[:, 2 * wide * share:, :] += dot(heads_ref[...].T, gm_ref[...].astype(bf16)).reshape(
        parts, share, width)

    @pl.when(step == pl.num_programs(0) - 1)
    def _():
        for c in range(wide):
            turned = down_ref[:, c * width:(c + 1) * width].T
            out_ref[:, c * share:(c + 1) * share, :] = turned.reshape(parts, share, width)


def mlp_grad_call(parts, n, gpre, act, cot, heads, gm, after):
    total, width = n.shape
    hidden = act.shape[1]
    rows = min(512, total)
    tall = lambda cols: row_spec((rows, cols), 0)
    packed = jax.ShapeDtypeStruct((parts, (hidden + hidden + width) // parts, width), f32)
    return staged_call(
        mlp_grad_kernel, "mlp_grad", total // rows,
        [n, gpre, act, cot, heads, gm],
        [tall(width), tall(hidden), tall(hidden), tall(width), tall(width), tall(width)],
        [packed], [whole_spec(packed)], (), after,
        2 * total * width * (2 * hidden + width), total * (hidden * 4 + width * 10),
        scratch=[pltpu.VMEM((width, hidden), f32)])


def in_grad_kernel(n_ref, d_ref, out_ref):
    @pl.when(pl.program_id(0) == 0)
    def _():
        out_ref[...] = jnp.zeros_like(out_ref)

    normed = n_ref[...].T
    for c in range(d_ref.shape[1] // TILE // 4 + 1):
        cols = slice(c * 4 * TILE, min((c + 1) * 4 * TILE, d_ref.shape[1]))
        out_ref[:, cols] += dot(normed, d_ref[:, cols])


def in_grad_call(n, d, after):
    total, width = n.shape
    rows = min(1024, total)
    out = jax.ShapeDtypeStruct((width, d.shape[1]), f32)
    return staged_call(
        in_grad_kernel, "in_grad", total // rows, [n, d],
        [row_spec((rows, width), 0), row_spec((rows, d.shape[1]), 0)], [out], [whole_spec(out)], (), after,
        2 * total * width * d.shape[1], total * width * 8)


def turn_kernel(piece, cuts, odd_ref, pq_ref, pk_ref, v_ref, dn_ref, gc_ref, gr_ref, st_ref, *rest):
    step = pl.program_id(0)
    back_ref, out_ref, gb_ref, ad_ref = rest[3 * len(cuts):]
    for number, (low, high) in enumerate(cuts):
        @pl.when((step >= low) & (step < high))
        def _(arrivals=rest[3 * number:3 * number + 3]):
            merged_state(0, odd_ref[0] > 0, arrivals, ad_ref)
    width = v_ref.shape[1]
    tiles = piece // TILE
    even_lane, odd_lane = pair_masks(piece)
    masks = (even_lane.astype(bf16), odd_lane.astype(bf16))
    smalls = [jnp.where(mask, 1.0 / HD, 0.0).astype(bf16) for mask in (even_lane, odd_lane)]
    diag = iota((TILE, TILE), 0) <= iota((TILE, TILE), 1)
    zero_tile = jnp.zeros((TILE, TILE), bf16)
    lane = iota((piece, TILE), 1)
    line_lane = iota((1, TILE), 1)
    cum_last = gc_ref[piece - 1:piece, :]
    blank = jnp.zeros((HD, PHI), bf16)
    odd_row = (iota((2 * TILE, TILE), 0) // HD) % 2
    col_sum = jnp.zeros((piece, TILE), f32)
    tail_sum = jnp.zeros((piece, TILE), f32)
    lead_sum = jnp.zeros((piece, TILE), f32)
    last_line = jnp.zeros((1, TILE), f32)
    row_parts = []

    def diagonal(blocks):
        return jnp.concatenate([
            jnp.concatenate([block, blank] if side == 0 else [blank, block], axis=1)
            for block, side in zip(blocks, (0, 1, 0, 1))], axis=0)

    def lane_sums(values, pair):
        high = values.astype(bf16)
        low = (values - high.astype(f32)).astype(bf16)
        chosen = (iota((2 * TILE, TILE), 1) == 2 * pair + odd_row).astype(bf16)
        return dot(jnp.concatenate([high, low], axis=1), chosen)

    for pair in range(PAIRS):
        cols = slice(pair * TILE, (pair + 1) * TILE)
        wide = slice(2 * pair * PHI, (2 * pair + 2) * PHI)
        value = v_ref[:, cols]
        both = dn_ref[:, 2 * pair * TILE:(2 * pair + 2) * TILE]
        states = state_pair(st_ref, 0, pair)
        adjoints = state_pair(ad_ref, 0, pair)
        state = jnp.concatenate(states, axis=0)
        adjoint = jnp.concatenate(adjoints, axis=0)
        tail = jnp.exp(pick(
            even_lane, cum_last[:, 2 * pair:2 * pair + 1] - gc_ref[:, 8 + 2 * pair:9 + 2 * pair],
            cum_last[:, 2 * pair + 1:2 * pair + 2] - gc_ref[:, 9 + 2 * pair:10 + 2 * pair]))
        lead = jnp.exp(pick(even_lane, gc_ref[:, 2 * pair:2 * pair + 1],
                            gc_ref[:, 2 * pair + 1:2 * pair + 2]))
        tail_value = tail * value.astype(f32)
        tail_small = tail * (1.0 / HD)
        far = dot_t(pk_ref[:, wide], diagonal(adjoints))
        tail_sum = tail_sum + lane_sums(tail_value * far[:, :TILE] + tail_small * far[:, TILE:], pair)
        far = tail * far[:, :TILE]
        lead_dn = lead * both[:, :TILE].astype(f32)
        lead_dd = (lead * (1.0 / HD)) * both[:, TILE:].astype(f32)
        outer = dot_t(pq_ref[:, wide], diagonal(states))
        lead_sum = lead_sum + lane_sums(lead_dn * outer[:, :TILE] + lead_dd * outer[:, TILE:], pair)
        tail_both = jnp.concatenate([tail_value.astype(bf16), tail_small.astype(bf16)], axis=1)
        lead_both = jnp.concatenate([lead_dn.astype(bf16), lead_dd.astype(bf16)], axis=1)
        probs = []
        angles_q = []
        angles_k = []
        for side in range(2):
            head = 2 * pair + side
            feats = slice(head * PHI, (head + 1) * PHI)
            phi_q = pq_ref[:, feats]
            phi_k = pk_ref[:, feats]
            mask = jnp.concatenate([masks[side], masks[side]], axis=1)
            value_h = jnp.concatenate([value * masks[side], smalls[side]], axis=1)
            scores = dot_t(phi_k, phi_q)
            dprob = dot_t(value_h, both)
            prob_lines = []
            ds_lines = []
            sums = [None] * tiles
            col_parts = []
            for a in range(tiles):
                delay = gc_ref[a * TILE:(a + 1) * TILE, 8 + head:9 + head]
                prob_line = []
                ds_line = []
                across = None
                for b in range(tiles):
                    if b < a:
                        prob_line.append(zero_tile)
                        ds_line.append(zero_tile)
                        continue
                    gap = gr_ref[0, head:head + 1, b * TILE:(b + 1) * TILE] - delay
                    if a == b:
                        gap = jnp.where(diag, gap, -1e30)
                    decay = jnp.exp(gap)
                    score = scores[a * TILE:(a + 1) * TILE, b * TILE:(b + 1) * TILE]
                    ds = dprob[a * TILE:(a + 1) * TILE, b * TILE:(b + 1) * TILE] * decay
                    energy = ds * score
                    across = energy if across is None else across + energy
                    down = jnp.sum(energy, axis=0, keepdims=True)
                    sums[b] = down if sums[b] is None else sums[b] + down
                    prob_line.append((decay * score).astype(bf16))
                    ds_line.append(ds.astype(bf16))
                col_parts.append(jnp.sum(across, axis=1, keepdims=True))
                prob_lines.append(jnp.concatenate(prob_line, axis=1))
                ds_lines.append(jnp.concatenate(ds_line, axis=1))
            probs.append(jnp.concatenate(prob_lines, axis=0))
            ds = jnp.concatenate(ds_lines, axis=0)
            row_parts.append(jnp.concatenate(sums, axis=1))
            col_sum = jnp.where(lane == head, jnp.concatenate(col_parts, axis=0), col_sum)
            dphi_k = dot(jnp.concatenate([ds, tail_both * mask], axis=1),
                         jnp.concatenate([phi_q, adjoint], axis=0))
            angles_k.append((dphi_k[:, :FEAT] * phi_k[:, FEAT:].astype(f32)
                             - dphi_k[:, FEAT:] * phi_k[:, :FEAT].astype(f32)).astype(bf16))
            dphi_q = t_dot(ds, phi_k) + dot(lead_both * mask, state)
            angles_q.append((dphi_q[:, :FEAT] * phi_q[:, FEAT:].astype(f32)
                             - dphi_q[:, FEAT:] * phi_q[:, :FEAT].astype(f32)).astype(bf16))
            cross = jnp.sum(st_ref[0, head * HD:(head + 1) * HD, :].astype(f32)
                            * ad_ref[0, head * HD:(head + 1) * HD, :].astype(f32),
                            axis=0, keepdims=True)
            cross = cross + (st_ref[0, HEADS * HD:STATE_ROWS, :].astype(f32)[head:head + 1]
                             * ad_ref[0, HEADS * HD:STATE_ROWS, :].astype(f32)[head:head + 1])
            last_line = jnp.where(line_lane == head, jnp.sum(cross, axis=1, keepdims=True), last_line)
        dn = both[:, :TILE]
        near = dot(jnp.concatenate(probs, axis=1),
                   jnp.concatenate([dn * masks[0], dn * masks[1]], axis=0))
        out_ref[:, 2 * width + pair * TILE:2 * width + (pair + 1) * TILE] = (near + far).astype(bf16)
        back = back_ref[pair]
        out_ref[:, cols] = dot(jnp.concatenate(angles_q, axis=1), back).astype(bf16)
        out_ref[:, width + pair * TILE:width + (pair + 1) * TILE] = dot(
            jnp.concatenate(angles_k, axis=1), back).astype(bf16)
    rows_block = jnp.concatenate(row_parts + [jnp.zeros((TILE - HEADS, piece), f32)], axis=0)
    grad_write = col_sum + tail_sum
    grad_cum = rows_block.T + lead_sum - grad_write
    last_line = (last_line * jnp.exp(cum_last) + jnp.sum(tail_sum, axis=0, keepdims=True))
    upper = (iota((piece, piece), 0) <= iota((piece, piece), 1)).astype(bf16)
    grad_gate = exact_sum(upper, grad_cum) + last_line
    logits = pltpu.roll(gc_ref[...], TILE - 16, 1)
    gate = jax.nn.sigmoid(logits)
    grad_logit = jnp.where(lane < HEADS, grad_gate * jax.nn.sigmoid(-logits) - gate * grad_write, 0.0)
    grad_logit = grad_logit.astype(bf16)
    out_ref[:, 3 * width:] = grad_logit

    @pl.when(step == 0)
    def _():
        gb_ref[...] = jnp.zeros_like(gb_ref)

    gb_ref[0:1, :] += jnp.sum(grad_logit.astype(f32), axis=0, keepdims=True)


def part_spec(block, low, high):
    rest = (0,) * (len(block) - 1)
    return pl.BlockSpec(
        block, lambda i, *_: (jnp.minimum(jnp.maximum(i - low, 0), high - low - 1),) + rest)


def turn_call(odd, pq, pk, v, dn, gc, gr, st, arrival_sets, back, piece, first, kept, after):
    total, width = v.shape
    tall = lambda cols: row_spec((piece, cols), first)
    cuts = []
    for arrivals in arrival_sets:
        low = cuts[-1][1] if cuts else 0
        cuts.append((low, low + arrivals[0].shape[0]))
    sents = cuts[-1][1]
    bias = jax.ShapeDtypeStruct((8, TILE), f32)
    return staged_call(
        functools.partial(turn_kernel, piece, cuts), "turn", sents,
        [pq, pk, v, dn, gc, gr, st, *(a for arrivals in arrival_sets for a in arrivals), back],
        [tall(HEADS * PHI), tall(HEADS * PHI), tall(width), tall(2 * width), tall(TILE),
         row_spec((1, 16, piece), first), row_spec((1, STATE_ROWS, PHI), first),
         *(part_spec((1, STATE_ROWS, PHI), *cut) for cut in cuts for _ in range(3)), whole_spec(back)],
        [jax.ShapeDtypeStruct((total, 3 * width + TILE), bf16), bias],
        [tall(3 * width + TILE), whole_spec(bias)],
        kept, after, sents * piece * piece * PHI, sents * piece * TILE,
        scratch=[pltpu.VMEM((1, STATE_ROWS, PHI), bf16)], prefetch=[odd])


def finish_kernel(x_ref, gm_ref, d_ref, gain_ref, w_ref, out_ref):
    grad_n = dot_t(d_ref[...], w_ref[...])
    gain = gain_ref[...]
    for tile in tiles_of(x_ref.shape[0], 128):
        x = x_ref[tile, :].astype(f32)
        center = x - jnp.mean(x, axis=1, keepdims=True)
        spread = jnp.mean(center * center, axis=1, keepdims=True)
        scale = lax.rsqrt(spread + norm_eps)
        xhat = center * scale
        gy = grad_n[tile] * gain
        first = jnp.mean(gy, axis=1, keepdims=True)
        second = jnp.mean(gy * xhat, axis=1, keepdims=True)
        out_ref[tile, :] = gm_ref[tile, :] + scale * (gy - first - xhat * second)


def finish_call(x, gm, d, gain, weights, rows, first, steps, kept, after):
    total, width = x.shape
    tall = lambda cols: row_spec((rows, cols), first)
    return staged_call(
        finish_kernel, "finish", steps, [x, gm, d, gain, weights],
        [tall(width), tall(width), tall(d.shape[1]), whole_spec(gain), whole_spec(weights)],
        [jax.ShapeDtypeStruct((total, width), f32)], [tall(width)], kept, after,
        2 * rows * steps * width * 3 * width, rows * steps * width * 20)


def mesh_bits():
    bits = []
    for axis in ("head", "dp"):
        size = lax.axis_size(axis)
        bit = 1
        while bit < size:
            bits.append((axis, bit))
            bit *= 2
    return bits


def swap(value, axis, bit):
    size = lax.axis_size(axis)
    return lax.ppermute(value, axis, [(i, i ^ bit) for i in range(size)])


def my_bit(axis, bit):
    return (lax.axis_index(axis) // bit) % 2


def tied(value, behind):
    if not behind:
        return value
    return lax.optimization_barrier((value, *behind))[0]


class Track:
    def __init__(self, rounds, count):
        self.rounds = rounds
        self.left = count
        self.behind = None

    def start(self):
        if self.left:
            self.left -= 1
            sent = self.rounds.send(self.behind)
            self.behind = []
            return [sent]
        return []

    def settle(self, behind):
        if self.behind is not None:
            self.behind = self.behind + [behind]

    def result(self):
        while self.left:
            self.start()
        return self.rounds.send(self.behind)


def gather_rounds(local, order):
    bits = mesh_bits()
    count = len(bits)
    held = local.reshape((1,) * count + local.shape)
    for place in order:
        axis, bit = bits[place]
        sent = held
        other = swap(sent, axis, bit)
        behind = yield sent
        other = tied(other, behind)
        dim = count - 1 - place
        held = jnp.where(my_bit(axis, bit) == 0, jnp.concatenate([held, other], axis=dim),
                         jnp.concatenate([other, held], axis=dim))
    while True:
        yield held.reshape((-1,) + local.shape[1:])


def two_parts(value):
    high = lax.reduce_precision(value, 8, 7)
    return high, lax.reduce_precision(value - high, 8, 7)


def scatter_rounds(total, everywhere, order):
    bits = mesh_bits()
    count = len(bits)
    lanes = everywhere.shape[1]
    wide = total.shape[2]
    held = total.reshape((2,) * count + total.shape[1:])
    for place in order:
        axis, bit = bits[place]
        mine = my_bit(axis, bit)
        dim = count - 1 - place
        send = lax.dynamic_slice_in_dim(held, 1 - mine, 1, dim)
        keep = lax.dynamic_slice_in_dim(held, mine, 1, dim)
        high, low = two_parts(everywhere)
        line = jnp.concatenate([high, low, jnp.zeros((1, wide - 2 * lanes), f32)], axis=1)
        line = jnp.concatenate([line, jnp.zeros((15, wide), f32)], axis=0)
        send = jnp.concatenate([send.reshape(-1, wide), line], axis=0).astype(bf16)
        other = swap(send, axis, bit)
        behind = yield send
        other = tied(other, behind).astype(f32)
        held = keep + other[:-16].reshape(keep.shape)
        everywhere = (high + low) + (other[-16:-15, :lanes] + other[-16:-15, lanes:2 * lanes])
    while True:
        yield held.reshape(total.shape[1:]), everywhere


def carry_rounds(local, reverse):
    size = lax.axis_size("head")
    chips = size // 2

    def hop(value, pairs):
        if reverse:
            pairs = [(size - 1 - a, size - 1 - b) for a, b in pairs]
        return lax.ppermute(value, "head", pairs)

    if chips == 2:
        near = hop(local, [(0, 1), (2, 3)])
        cross = hop(local, [(1, 2), (0, 3)])
        behind = yield local
        near, cross = tied((near, cross), behind)
        swapped = hop(cross, [(2, 3), (3, 2)])
        behind = yield cross
        swapped = tied(swapped, behind)
        while True:
            yield [near, cross, swapped]
    near = hop(local, [(2 * c, 2 * c + 1) for c in range(chips)])
    behind = yield local
    ends = join_states(local, tied(near, behind))
    far = None
    late = None
    for c in range(chips - 1):
        come = hop(ends, [(2 * c + 1, 2 * c + 2)])
        behind = yield ends
        come = tied(come, behind)
        relay = hop(come, [(2 * c + 2, 2 * c + 3)])
        far = come if far is None else far + come
        late = relay if late is None else late + relay
        behind = yield come
        relay = tied(relay, behind)
        if c < chips - 2:
            ends = join_states(local, join_states(near, late))
    while True:
        yield [near, far, late]


def feature_tables(projection):
    turns = projection * (1.0 / (2.0 * math.pi))
    high = lax.reduce_precision(turns, 8, 7)
    low = turns - high

    def blocks(part):
        paired = part.reshape(PAIRS, 2, HD, FEAT)
        blank = jnp.zeros_like(paired[:, 0])
        return jnp.concatenate([
            jnp.concatenate([paired[:, 0], blank], axis=2),
            jnp.concatenate([blank, paired[:, 1]], axis=2)], axis=1)

    forward = jnp.concatenate([blocks(high), blocks(low)], axis=1).astype(bf16)
    backward = blocks(projection).transpose(0, 2, 1).astype(bf16)
    return forward, backward


def body(tokens, lengths, feature_proj, first_gain, query_weight, key_weight, value_weight, gate_weight,
         gate_bias, output_weight, second_gain, up_weight, down_weight, cotangent):
    slots = lengths.shape[0]
    total, width = tokens.shape
    piece = total // slots
    head_index = lax.axis_index("head")
    rows_local = query_weight.shape[0]
    devices = lax.axis_size("dp") * lax.axis_size("head")
    hidden = up_weight.shape[1]
    gains = jnp.stack([first_gain, second_gain], axis=1)
    gate_lanes = jnp.concatenate(
        [gate_weight, gate_weight, gate_weight, gains,
         jnp.zeros((rows_local, TILE - 3 * HEADS - 2), bf16)], axis=1)
    packed = jnp.concatenate([query_weight, key_weight, value_weight, gate_lanes], axis=1)
    count = len(mesh_bits())
    place_order = list(reversed(range(count)))
    first_gather = Track(gather_rounds(packed, place_order), count)
    first_gather.start()
    begun = first_gather.start()
    wide = hidden // width
    up_mixed = tied(up_weight, begun).reshape(rows_local, devices, wide, rows_local).transpose(0, 2, 1, 3)
    down_mixed = tied(down_weight, begun).reshape(wide, rows_local, width).transpose(1, 0, 2)
    middle_weights = lax.all_gather(
        jnp.concatenate([up_mixed.reshape(rows_local, hidden), tied(output_weight, begun),
                         down_mixed.reshape(rows_local, hidden)], axis=1),
        ("dp", "head"), axis=0, tiled=True)
    first_full = first_gather.result()
    gain_lanes = first_full[:, 3 * width + 3 * HEADS:3 * width + 3 * HEADS + 2].astype(f32)
    gain_one = gain_lanes[:, 0][None, :]
    gain_two = gain_lanes[:, 1][None, :]
    gate_b = jnp.concatenate([gate_bias] * 3 + [jnp.zeros((TILE - 3 * HEADS,), f32)])[None, :]
    proj, back = feature_tables(feature_proj)
    lane = jnp.arange(TILE)
    seg = (lane[:, None] // HD == lane[None, :] // HD).astype(bf16)
    seg = jnp.concatenate([seg, seg], axis=0)

    lead_size = slots * 7 // 16
    sizes = [lead_size, slots - lead_size]
    firsts = [0, lead_size]
    chunks = len(sizes)
    chips = lax.axis_size("head") // 2
    hops = 2 if chips == 2 else 2 * chips - 1

    def beside(tracks, call, through=()):
        sent = []
        for track in tracks:
            sent += track.start()
        out = call(sent)
        for track in (*tracks, *through):
            track.settle(out[-1])
        return out

    states = []
    kept = ()
    for k in range(chunks):
        *kept, local = beside(states[k - 1:k] if k else (), lambda after: key_call(
            tokens, gain_one, first_full, gate_b, proj, piece, 1, sizes[k], firsts[k], kept,
            after + ([] if k else [back, seg])), states[:max(k - 1, 0)])
        states.append(Track(carry_rounds(local, False), hops))
    normed, pk, v, gc, gr = kept
    (pq,) = beside(states[-1:], lambda after: query_call(normed, first_full, proj, after), states[:-1])

    bound = jnp.concatenate([lengths - head_index * piece, (head_index % 2)[None]])
    odd_back = (1 - head_index % 2)[None]
    adjoints = []
    kept = ()
    parts = [[(0, sizes[0])], [(0, slots // 4), (slots // 4, sizes[1])]]
    for k in range(chunks):
        arrivals = states[k].result()
        out = beside(adjoints, lambda after: middle_call(
            bound, tokens, cotangent, pq, pk, v, gc, gr, arrivals, gain_two, middle_weights, seg, piece, 1,
            True, parts[k], sizes[k], firsts[k], kept, after), states[k + 1:])
        kept = out[:8]
        adjoints += [Track(carry_rounds(local, True), hops) for local in out[8:]]
    mixed, gm, heads_low, n_two, act, gpre, dn, state_in = kept
    (mlp_grad,) = beside(adjoints[:2], lambda after: mlp_grad_call(
        devices, n_two, gpre, act, cotangent, heads_low, gm, after))
    arrivals = adjoints[0].result()
    begun = adjoints[1].start()
    mlp_part = lax.psum_scatter(tied(mlp_grad, arrivals[-1:] + begun),
                                ("dp", "head"), scatter_dimension=0, tiled=False)
    dqkv, bias_part = beside(adjoints[2:], lambda after: turn_call(
        odd_back, pq, pk, v, dn, gc, gr, state_in, [arrivals], back, piece, 0, (), after + begun),
        adjoints[1:2])
    late_arrivals = [adjoints[1].result(), adjoints[2].result()]
    dqkv, grad_bias = turn_call(
        odd_back, pq, pk, v, dn, gc, gr, state_in, late_arrivals, back, piece, sizes[0], [dqkv], [])
    grad_bias = grad_bias + bias_part
    (in_grad,) = in_grad_call(normed, dqkv, ())
    in_sum = Track(scatter_rounds(in_grad.reshape((devices, -1) + in_grad.shape[1:]), grad_bias[0:1],
                                  list(range(count))), count)
    kept = ()
    blocks = 8 if total % 4096 == 0 else 4
    cuts = [0, (3 * blocks + 4) // 8, (6 * blocks + 4) // 8, blocks]
    for k in range(3):
        kept = beside([in_sum], lambda after: finish_call(
            tokens, gm, dqkv, gain_one, first_full, total // blocks, cuts[k], cuts[k + 1] - cuts[k], kept,
            after + ([mlp_part] if k == 2 else [])))
    grad_tokens = kept[0]
    last, grad_bias = in_sum.result()
    grad_bias = grad_bias[0, :HEADS]
    split = wide * rows_local
    grad_down = mlp_part[:split]
    grad_up = mlp_part[split:2 * split].reshape(wide, rows_local, devices, rows_local).transpose(
        1, 2, 0, 3).reshape(rows_local, hidden)
    grad_output = mlp_part[2 * split:]
    grad_gate = last[:, 3 * width:3 * width + HEADS]
    mine = jnp.concatenate([query_weight, key_weight, value_weight, gate_weight], axis=1).astype(f32)
    grad_first_gain = jnp.sum(mine * last[:, :3 * width + HEADS], axis=1) / first_gain.astype(f32)
    grad_second_gain = jnp.sum(up_weight.astype(f32) * grad_up, axis=1) / second_gain.astype(f32)
    return (
        mixed,
        grad_tokens,
        grad_first_gain,
        last[:, :width],
        last[:, width:2 * width],
        last[:, 2 * width:3 * width],
        grad_gate,
        grad_bias,
        grad_output,
        grad_second_gain,
        grad_up,
        grad_down,
    )


def solution(mesh):
    split = P(("dp", "head"), None)
    line = P(("dp", "head"))
    return jax.shard_map(
        body,
        mesh=mesh,
        in_specs=(split, P("dp"), P(), line, split, split, split, split, P(), split, line, split, split,
                  split),
        out_specs=(split, split, line, split, split, split, split, P(), split, line, split, split),
        check_vma=False,
    )
```
